512 devices in a mesh: slab: 16 (over z, core), func: 32 (over y, x).
Axes of the slice: x: 4, y: 8, z: 8, core: 2. Of those that a mesh axis runs over, the one named last changes fastest.
Arguments:
- coefficients: float32 [4096, 16, 1024], P(('slab', 'func')), may hold values from -0.6 to 0.6
- offsets: int32 [4096, 3], P(('slab', 'func')), may hold values from 0 to 255, as said below
- extents: int32 [4096, 3], P(('slab', 'func')), may hold values from 8 to 32, as said below
- occupancy: int32 [4096], P(('slab', 'func')), may hold values from 0 to 2
- potential: float32 [128, 32768], P('slab', 'func'), may hold values from -6 to 6
Outputs:
- density: float32 [128, 32768], P('slab', 'func')
- applied: float32 [4096, 16, 1024], P(('slab', 'func'))
The draws below stay inside these ranges and needn't reach their ends.
Inputs may be any that keep to these rules, and one draw needn't show every extreme that they name: Function r has its home slab r // 256 and its home band j = (r // 8) % 32: offsets[r, 0] lies in [home * 8, home * 8 + 8), offsets[r, 1] in [j * 8, j * 8 + 8), and offsets[r, 2] is at most 96. extents[r] along z, y, x lie in [8, 16], [16, 32] and [16, 32].
All inputs are finite; a program needn't handle non-finite values.
Results may differ from the reference program's by a relative error of at most 0.0003.
Values sent between devices are 32-bit elements; how exact they have to be, the bound alone decides.
A program may use at most 64 MiB of HBM per device.

```python
import jax
import jax.numpy as jnp
import numpy as np
from jax import lax

BZ = 16
BY = 32
BX = 32
CZ = 8
RY = 8
NX = 128
F_DEV = 8
NZ = 128
NY = 256
SLAB_FUNCS = 256
FUNCS = 4096


def draw_offsets(key, part):
    key = jax.random.fold_in(key, 11)
    keys = jax.random.split(key, 3)
    row_index = jnp.arange(FUNCS)
    home = row_index // SLAB_FUNCS
    band = row_index // F_DEV % (SLAB_FUNCS // F_DEV)
    depth = home * CZ + jax.random.randint(keys[0], (FUNCS,), 0, CZ)
    rows_at = band * RY + jax.random.randint(keys[1], (FUNCS,), 0, RY)
    columns_at = jax.random.randint(keys[2], (FUNCS,), 0, NX - BX + 1)
    drawn = jnp.stack([depth, rows_at, columns_at], axis=1).astype(jnp.int32)
    drawn = drawn.at[0].set(jnp.zeros((3,), jnp.int32))
    last_row = jnp.array([NZ - 1, NY - 1, NX - BX], jnp.int32)
    return drawn.at[FUNCS - 1].set(last_row)


def draw_extents(key, part):
    key = jax.random.fold_in(key, 23)
    keys = jax.random.split(key, 3)
    depth = jax.random.randint(keys[0], (FUNCS,), BZ // 2, BZ + 1)
    rows_live = jax.random.randint(keys[1], (FUNCS,), BY // 2, BY + 1)
    columns_live = jax.random.randint(keys[2], (FUNCS,), BX // 2, BX + 1)
    return jnp.stack([depth, rows_live, columns_live], axis=1).astype(jnp.int32)


def touch_ends(entries, stream_key, least, top_value):
    longest = entries.shape.index(max(entries.shape))
    spots = []
    for shift in (0, 1):
        where = [jax.random.randint(jax.random.fold_in(stream_key, axis), (), 0, length) for axis, length in enumerate(entries.shape)]
        where[longest] = (where[longest] + shift) % entries.shape[longest]
        spots.append(tuple(where))
    return entries.at[spots[0]].set(least).at[spots[1]].set(top_value)


def levels(stream_key, extent, pieces, low, top_value):
    gain = 1.0
    for axis_at, shards_of in pieces:
        draws = jax.random.uniform(jax.random.fold_in(jax.random.fold_in(stream_key, 6), axis_at), (shards_of,), jnp.float32, low / len(pieces), top_value / len(pieces))
        gain = gain * jnp.repeat(jnp.exp(draws), extent[axis_at] // shards_of).reshape((-1,) + (1,) * (len(extent) - 1 - axis_at))
    return gain


def noise(key, extent, width, reach, pieces=(), held_as=jnp.bfloat16):
    factor_of = levels(key, extent, pieces, -0.22, 0.18) if pieces else 1.0
    values = jax.random.normal(key, extent, jnp.float32) * width * factor_of
    return jnp.minimum(jnp.maximum(values, -reach), reach).astype(held_as)


def setup_inputs(seed: int = 0) -> dict:
    streams_of = jax.random.split(jax.random.key(seed), 6)
    coefficients = noise(streams_of[0], (FUNCS, BZ, BY * BX), 0.1, 0.6, ((0, 512),), jnp.float32)
    offsets = draw_offsets(jax.random.fold_in(streams_of[5], 71), 0)
    extents = draw_extents(jax.random.fold_in(streams_of[5], 71), 0)
    occupancy = touch_ends(jax.random.randint(streams_of[3], (FUNCS,), 0, 3), jax.random.fold_in(streams_of[3], 1), 0, 2).astype(jnp.int32)
    potential = noise(streams_of[4], (NZ, NY * NX), 1.0, 6.0, ((0, 16), (1, 32)), jnp.float32)
    return {"coefficients": coefficients, "offsets": offsets, "extents": extents, "occupancy": occupancy, "potential": potential}


magic_taps = np.array([8.4334247333529341e-7, -1.2905572013420610e-5, 8.7629844762105596e-5, -3.0158038132690463e-4, 1.7472371367299390e-3, -9.4204703020108039e-3, 2.3738214637249424e-2, 6.1262589583120798e-2, 9.9404156978340040e-1, -6.0489528919698352e-2, -2.1030251609303814e-2, 1.3372634148547948e-2, -3.4412814449349386e-3, 4.9443227688689919e-4, -5.1859868811734329e-5, 2.7273449291197966e-6])


def filter_matrix(length):
    row_index = jnp.arange(length)[:, None]
    column_index = jnp.arange(length)[None, :]
    distance = column_index - row_index
    table = jnp.zeros((length, length), jnp.float32)
    for filter_tap in range(16):
        table = table + jnp.where(distance == filter_tap - 8, jnp.float32(magic_taps[filter_tap]), jnp.float32(0.0))
    return table


def decode(block, filter_depth, filter_rows, filter_columns):
    highest = lax.Precision.HIGHEST
    volume = block.reshape(block.shape[0], BZ, BY, BX)
    volume = jnp.einsum('ab,fbyx->fayx', filter_depth, volume, precision=highest)
    volume = jnp.einsum('ab,fzbx->fzax', filter_rows, volume, precision=highest)
    return jnp.einsum('ab,fzyb->fzya', filter_columns, volume, precision=highest)


def encode(volume, filter_depth, filter_rows, filter_columns):
    highest = lax.Precision.HIGHEST
    volume = jnp.einsum('ba,fbyx->fayx', filter_depth, volume, precision=highest)
    volume = jnp.einsum('ba,fzbx->fzax', filter_rows, volume, precision=highest)
    volume = jnp.einsum('ba,fzyb->fzya', filter_columns, volume, precision=highest)
    return volume.reshape(volume.shape[0], BZ, BY * BX)


def box_mask(extents):
    depth = jnp.arange(BZ)[None, :, None, None] < extents[:, 0][:, None, None, None]
    rows_ok = jnp.arange(BY)[None, None, :, None] < extents[:, 1][:, None, None, None]
    columns_ok = jnp.arange(BX)[None, None, None, :] < extents[:, 2][:, None, None, None]
    return (depth & rows_ok & columns_ok).astype(jnp.float32)


def reference(coefficients, offsets, extents, occupancy, potential):
    filter_depth = filter_matrix(BZ)
    filter_rows = filter_matrix(BY)
    filter_columns = filter_matrix(BX)
    field = potential.reshape(NZ, NY, NX)
    field_wrapped = jnp.concatenate([field, field[:BZ]], axis=0)
    field_wrapped = jnp.concatenate([field_wrapped, field_wrapped[:, :BY]], axis=1)
    blocks = FUNCS // F_DEV
    coef_blocks = coefficients.reshape(blocks, F_DEV, BZ, BY * BX)
    offset_blocks = offsets.reshape(blocks, F_DEV, 3)
    extent_blocks = extents.reshape(blocks, F_DEV, 3)
    occupancy_blocks = occupancy.reshape(blocks, F_DEV)

    def one_block(extended, inputs):
        block, corners, sizes, weights = inputs
        orbital = decode(block, filter_depth, filter_rows, filter_columns) * box_mask(sizes)
        boxes = jax.vmap(lambda corner: lax.dynamic_slice(field_wrapped, (corner[0], corner[1], corner[2]), (BZ, BY, BX)))(corners)
        result = encode(boxes * orbital, filter_depth, filter_rows, filter_columns)
        terms = weights.astype(jnp.float32)[:, None, None, None] * orbital * orbital

        def add_one(index, accum_field):
            corner = corners[index]
            current = lax.dynamic_slice(accum_field, (corner[0], corner[1], corner[2]), (BZ, BY, BX))
            return lax.dynamic_update_slice(accum_field, current + terms[index], (corner[0], corner[1], corner[2]))

        extended = lax.fori_loop(0, F_DEV, add_one, extended)
        return extended, result

    start = jnp.zeros((NZ + BZ, NY + BY, NX), jnp.float32)
    extended, applied = lax.scan(one_block, start, (coef_blocks, offset_blocks, extent_blocks, occupancy_blocks))
    folded = extended[:NZ].at[:BZ].add(extended[NZ:])
    density = folded[:, :NY].at[:, :BY].add(folded[:, NY:])
    return density.reshape(NZ, NY * NX), applied.reshape(FUNCS, BZ, BY * BX)
```

```python
import jax
import jax.numpy as jnp
import numpy as np
from jax import lax
from jax.experimental import pallas as pl
from jax.experimental.pallas import tpu as pltpu
from jax.sharding import PartitionSpec as P

BZ = 16
BY = 32
BX = 32
CZ = 8
RY = 8
NX = 128
FD = 8
WZ = 24
WY = 40
LT = 256
MESH = pl.DeviceIdType.MESH
F32 = jnp.float32
BF16 = jnp.bfloat16
PAIRS = [(ds, db) for db in range(5) for ds in (2, 1, 0) if (ds, db) != (0, 0)]
SLOT = {pair: slot for slot, pair in enumerate(PAIRS)}

magic_taps = np.array(
    [
        8.433424733352934e-07,
        -1.290557201342061e-05,
        8.76298447621056e-05,
        -0.00030158038132690465,
        0.001747237136729939,
        -0.009420470302010804,
        0.023738214637249424,
        0.0612625895831208,
        0.9940415697834004,
        -0.06048952891969835,
        -0.021030251609303816,
        0.013372634148547948,
        -0.0034412814449349387,
        0.0004944322768868992,
        -5.185986881173433e-05,
        2.7273449291197967e-06,
    ]
).astype(np.float32)


def tap(distance):
    inside = (distance >= -8) & (distance <= 7)
    return np.where(inside, magic_taps[np.clip(distance + 8, 0, 15)], 0.0).astype(np.float64)


def plane_tiles(backward):
    row = np.arange(LT)[:, None]
    col = np.arange(LT)[None, :]
    tiles = []
    for step in (-1, 0, 1):
        if backward:
            along_y = tap(col // BX - row // BX - 8 * step)
            along_x = tap(col % BX - row % BX)
        else:
            along_y = tap(8 * step + row // BX - col // BX)
            along_x = tap(row % BX - col % BX)
        full = along_y * along_x
        tiles.append(full.astype(np.float32))
    return np.stack(tiles)


def split(value):
    high = value.astype(BF16)
    return high, (value - high.astype(F32)).astype(BF16)


def dot(a, b):
    return jnp.dot(a, b, preferred_element_type=F32)


def plane_filter(high, low, tiles, out):
    def pair(first, last, step):
        big, small = split(tiles[step + 1])
        return dot(high[first:last], big) + dot(low[first:last], big) + dot(high[first:last], small)

    out[...] = pair(0, 512, 0)
    out[0:384] += pair(128, 512, 1)
    out[128:512] += pair(0, 384, -1)


def tap_select(distance):
    value = jnp.zeros(distance.shape, F32)
    for t in range(16):
        value = jnp.where(distance == t - 8, F32(magic_taps[t]), value)
    return value


def work(
    off, ext, occ, coef_hbm, pot, kd_hbm, ke_hbm, app_hbm, den,
    coef, kd, ke, high, low, grid, zh, zl, th, tl, orb, term, window, acc, got, prod, app,
    load_sem, psend, precv, dsend, drecv,
):
    s = lax.axis_index("slab")
    j = lax.axis_index("func")

    def device(a, b):
        return (lax.rem(s + a + 16, 16), lax.rem(j + b + 32, 32))

    load_c = pltpu.make_async_copy(coef_hbm, coef, load_sem.at[0])
    load_d = pltpu.make_async_copy(kd_hbm, kd, load_sem.at[1])
    load_e = pltpu.make_async_copy(ke_hbm, ke, load_sem.at[2])
    load_c.start()
    load_d.start()
    load_e.start()
    barrier = pltpu.get_barrier_semaphore()
    for ds, db in PAIRS:
        pl.semaphore_signal(barrier, 1, device_id=device(ds, db), device_id_type=MESH)
        pl.semaphore_signal(barrier, 1, device_id=device(-ds, -db), device_id_type=MESH)

    dz = [off[0, f] & (CZ - 1) for f in range(FD)]
    dy = [off[1, f] & (RY - 1) for f in range(FD)]
    ox = [off[2, f] for f in range(FD)]
    for y in range(RY):
        window[0, y] = pot[:, y * NX : (y + 1) * NX]

    a_index = lax.broadcasted_iota(jnp.int32, (WZ, 128), 0)
    c_index = lax.broadcasted_iota(jnp.int32, (WZ, 128), 1)
    for f in range(0, FD, 2):
        parts = []
        for e in (f, f + 1):
            b = c_index - 16 * e
            a = a_index - dz[e]
            valid = (b >= 0) & (b < BZ) & (a >= 0) & (a < ext[0, e])
            parts.append(jnp.where(valid, tap_select(b - a), 0.0))
        h, l = split(jnp.concatenate(parts, axis=0))
        zh[f * WZ : (f + 2) * WZ] = h
        zl[f * WZ : (f + 2) * WZ] = l
    r_index = lax.broadcasted_iota(jnp.int32, (128, 256), 0)
    col = lax.broadcasted_iota(jnp.int32, (8, 256), 1)
    base = jnp.zeros((8, 256), jnp.int32)
    layer = jnp.full((8, 256), -1000, jnp.int32)
    top = jnp.zeros((8, 256), jnp.int32)
    for f in range(FD):
        mine = (col >= WZ * f) & (col < WZ * (f + 1))
        base = jnp.where(mine, 16 * f, base)
        layer = jnp.where(mine, col - WZ * f - dz[f], layer)
        top = jnp.where(mine, ext[0, f], top)
    tb = r_index - jnp.tile(base, (16, 1))
    ta = jnp.tile(layer, (16, 1))
    valid = (tb >= 0) & (tb < BZ) & (ta >= 0) & (ta < jnp.tile(top, (16, 1)))
    h, l = split(jnp.where(valid, tap_select(tb - ta), 0.0))
    th[...] = h
    tl[...] = l
    zero = jnp.zeros((WZ, NX), F32)
    for f in range(FD):
        for k in (0, 1, 10, 11):
            term[f, k] = zero
    for k in range(8):
        prod[k, 192:256] = jnp.zeros((64, NX), F32)

    pl.semaphore_wait(barrier, 2 * len(PAIRS))
    pot_copies = []
    for ds, db in PAIRS:
        copy = pltpu.make_async_remote_copy(
            window.at[0, pl.ds(0, RY)],
            window.at[ds, pl.ds(RY * db, RY)],
            psend.at[SLOT[ds, db]],
            precv.at[SLOT[ds, db]],
            device_id=device(-ds, -db),
            device_id_type=MESH,
        )
        copy.start()
        pot_copies.append(copy)

    load_c.wait()
    for t in range(4):
        h, l = split(coef[:, t * LT : (t + 1) * LT])
        high[t * 128 : (t + 1) * 128] = h
        low[t * 128 : (t + 1) * 128] = l
    load_d.wait()
    plane_filter(high, low, kd, grid)

    lane = lax.broadcasted_iota(jnp.int32, (WZ, NX), 1)
    lane_x = lane & 31
    lane_y = lane >> 5
    for t in range(4):
        gh, gl = split(grid[t * 128 : (t + 1) * 128])
        placed = dot(zh[...], gh) + dot(zl[...], gh) + dot(zh[...], gl)
        for f in range(FD):
            live_x = lane_x < ext[2, f]
            weight = occ[f].astype(F32)
            for half in range(2):
                k = 2 * t + half
                live = live_x & (lane_y < ext[1, f] - 4 * k)
                value = jnp.where(live, placed[f * WZ : (f + 1) * WZ, half * NX : (half + 1) * NX], 0.0)
                orb[f, k] = value
                term[f, k + 2] = weight * (value * value)

    den_copies = []
    inside = [(lane >= ox[f]) & (lane < ox[f] + BX) for f in range(FD)]
    for db in range(5):

        def one_row(step, carry, db=db):
            r = db * RY + step
            total = jnp.zeros((WZ, NX), F32)
            for f in range(FD):
                at = r - dy[f] + 8
                turn = (ox[f] + 128 - 32 * (at & 3)) & 127
                total = total + jnp.where(inside[f], pltpu.roll(term[f, at >> 2], turn, 1), 0.0)
            for ds in range(3):
                acc[ds, r] = total[ds * CZ : (ds + 1) * CZ]
            return carry

        lax.fori_loop(0, RY, one_row, 0, unroll=True)
        for ds in (2, 1, 0):
            if (ds, db) == (0, 0):
                continue
            slot = SLOT[ds, db]
            copy = pltpu.make_async_remote_copy(
                acc.at[ds, pl.ds(RY * db, RY)],
                got.at[slot],
                dsend.at[slot],
                drecv.at[slot],
                device_id=device(ds, db),
                device_id_type=MESH,
            )
            copy.start()
            den_copies.append(copy)

    for copy in pot_copies:
        copy.wait_recv()

    def encode_plane(k, carry):
        for f in range(FD):
            box = jnp.zeros((WZ, NX), F32)
            for g in range(4):
                row = window[:, pl.ds(4 * k + g + dy[f], 1)].reshape(WZ, NX)
                box = jnp.where(lane_y == g, pltpu.roll(row, (128 + 32 * g - ox[f]) & 127, 1), box)
            prod[k, f * WZ : (f + 1) * WZ] = box * orb[f, k]
        return carry

    lax.fori_loop(0, 8, encode_plane, 0)
    load_e.wait()
    for t in range(4):
        ph, p_low = split(jnp.concatenate([prod[2 * t], prod[2 * t + 1]], axis=1))
        back = dot(th[...], ph) + dot(tl[...], ph) + dot(th[...], p_low)
        h, l = split(back)
        high[t * 128 : (t + 1) * 128] = h
        low[t * 128 : (t + 1) * 128] = l
    plane_filter(high, low, ke, grid)
    for t in range(4):
        app[:, t * LT : (t + 1) * LT] = grid[t * 128 : (t + 1) * 128]
    store = pltpu.make_async_copy(app, app_hbm, load_sem.at[3])
    store.start()
    for copy in den_copies:
        copy.wait_recv()
    for y in range(RY):
        total = acc[0, y]
        for slot in range(len(PAIRS)):
            total = total + got[slot, y]
        den[:, y * NX : (y + 1) * NX] = total
    for copy in pot_copies:
        copy.wait_send()
    for copy in den_copies:
        copy.wait_send()
    store.wait()


def hand_over(app_in, den_in, app_out, den_out):
    app_out[...] = app_in[...]
    den_out[...] = den_in[...]


def per_device(coefficients, offsets, extents, occupancy, potential):
    any_space = pl.BlockSpec(memory_space=pl.ANY)
    hbm = pl.BlockSpec(memory_space=pltpu.HBM)
    scalar = pl.BlockSpec(memory_space=pltpu.SMEM)
    whole = pl.BlockSpec(memory_space=pltpu.VMEM)
    n = len(PAIRS)
    app, den = pl.pallas_call(
        work,
        out_shape=(
            jax.ShapeDtypeStruct((FD * BZ, BY * BX), F32),
            jax.ShapeDtypeStruct((CZ, RY * NX), F32),
        ),
        in_specs=[scalar, scalar, scalar, hbm, whole, hbm, hbm],
        out_specs=(any_space, whole),
        scratch_shapes=[
            pltpu.VMEM((128, 1024), F32),
            pltpu.VMEM((3, LT, LT), F32),
            pltpu.VMEM((3, LT, LT), F32),
            pltpu.VMEM((512, LT), BF16),
            pltpu.VMEM((512, LT), BF16),
            pltpu.VMEM((512, LT), F32),
            pltpu.VMEM((192, 128), BF16),
            pltpu.VMEM((192, 128), BF16),
            pltpu.VMEM((128, 256), BF16),
            pltpu.VMEM((128, 256), BF16),
            pltpu.VMEM((FD, 8, WZ, NX), F32),
            pltpu.VMEM((FD, 12, WZ, NX), F32),
            pltpu.VMEM((3, WY, CZ, NX), F32),
            pltpu.VMEM((3, WY, CZ, NX), F32),
            pltpu.VMEM((n, RY, CZ, NX), F32),
            pltpu.VMEM((8, 256, NX), F32),
            pltpu.VMEM((128, 1024), F32),
            pltpu.SemaphoreType.DMA((4,)),
            pltpu.SemaphoreType.DMA((n,)),
            pltpu.SemaphoreType.DMA((n,)),
            pltpu.SemaphoreType.DMA((n,)),
            pltpu.SemaphoreType.DMA((n,)),
        ],
        compiler_params=pltpu.CompilerParams(
            collective_id=0, has_side_effects=True, vmem_limit_bytes=63 * 1024 * 1024
        ),
        name="local_potential",
    )(
        offsets.T,
        extents.T,
        occupancy,
        coefficients.reshape(FD * BZ, BY * BX),
        potential,
        jnp.asarray(plane_tiles(False)),
        jnp.asarray(plane_tiles(True)),
    )
    app, den = pl.pallas_call(
        hand_over,
        out_shape=(
            jax.ShapeDtypeStruct((FD * BZ, BY * BX), F32),
            jax.ShapeDtypeStruct((CZ, RY * NX), F32),
        ),
        in_specs=[whole, whole],
        out_specs=(whole, whole),
        name="hand_over",
    )(app, den)
    return den, app.reshape(FD, BZ, BY * BX)


def solution(mesh):
    in_specs = (
        P(("slab", "func"), None, None),
        P(("slab", "func"), None),
        P(("slab", "func"), None),
        P(("slab", "func")),
        P("slab", "func"),
    )
    out_specs = (P("slab", "func"), P(("slab", "func"), None, None))
    return jax.shard_map(
        per_device, mesh=mesh, in_specs=in_specs, out_specs=out_specs, check_vma=False
    )
```

```python
import jax
import jax.numpy as jnp
import numpy as np
from jax import lax
from jax.experimental import pallas as pl
from jax.experimental.pallas import tpu as pltpu
from jax.sharding import PartitionSpec as P

BZ = 16
BY = 32
BX = 32
CZ = 8
RY = 8
NX = 128
FD = 8
WZ = 24
WY = 40
LT = 256
MESH = pl.DeviceIdType.MESH
F32 = jnp.float32
BF16 = jnp.bfloat16
AROUND = [(2, 0)] + [(0, db) for db in (4, 3, 2, 1)]

magic_taps = np.array(
    [
        8.433424733352934e-07,
        -1.290557201342061e-05,
        8.76298447621056e-05,
        -0.00030158038132690465,
        0.001747237136729939,
        -0.009420470302010804,
        0.023738214637249424,
        0.0612625895831208,
        0.9940415697834004,
        -0.06048952891969835,
        -0.021030251609303816,
        0.013372634148547948,
        -0.0034412814449349387,
        0.0004944322768868992,
        -5.185986881173433e-05,
        2.7273449291197967e-06,
    ]
).astype(np.float32)


def tap(distance):
    inside = (distance >= -8) & (distance <= 7)
    return np.where(inside, magic_taps[np.clip(distance + 8, 0, 15)], 0.0).astype(np.float64)


def plane_tiles(backward):
    row = np.arange(LT)[:, None]
    col = np.arange(LT)[None, :]
    tiles = []
    for step in (-1, 0, 1):
        if backward:
            along_y = tap(col // BX - row // BX - 8 * step)
            along_x = tap(col % BX - row % BX)
        else:
            along_y = tap(8 * step + row // BX - col // BX)
            along_x = tap(row % BX - col % BX)
        full = along_y * along_x
        tiles.append(full.astype(np.float32))
    return np.stack(tiles)


def split(value):
    high = value.astype(BF16)
    return high, (value - high.astype(F32)).astype(BF16)


def dot(a, b):
    return jnp.dot(a, b, preferred_element_type=F32)


def plane_filter(high, low, tiles, out):
    def pair(first, last, step):
        big, small = split(tiles[step + 1])
        return dot(high[first:last], big) + dot(low[first:last], big) + dot(high[first:last], small)

    out[...] = pair(0, 512, 0)
    out[0:384] += pair(128, 512, 1)
    out[128:512] += pair(0, 384, -1)


def layer_matrices():
    row = np.arange(FD * BZ)[:, None]
    col = np.arange(FD * BZ)[None, :]
    full = np.where(row // BZ == col // BZ, tap(col - row), 0.0).astype(np.float32)
    return np.stack([full, full.T])


def work(
    off_hbm, ext_hbm, occ_hbm, coef_hbm, pot_hbm, kd_hbm, ke_hbm, z_hbm, app, den,
    coef, kd, ke, zm, tiles, pair, high, low, grid, zd, ze, orb, term, seen, window, acc, got, prod,
    off, ext, occ, pot, load_sem, send_sem, recv_sem, late,
):
    s = lax.axis_index("slab")
    j = lax.axis_index("func")

    def device(a, b):
        return (lax.rem(s + a + 16, 16), lax.rem(j + b + 32, 32))

    load_c = pltpu.make_async_copy(coef_hbm, coef, load_sem.at[0])
    load_d = pltpu.make_async_copy(kd_hbm, kd, load_sem.at[1])
    load_z = pltpu.make_async_copy(z_hbm, zm, load_sem.at[2])
    load_e = pltpu.make_async_copy(ke_hbm, ke, load_sem.at[3])
    small = [
        pltpu.make_async_copy(source, target, load_sem.at[5 + k])
        for k, (source, target) in enumerate([(off_hbm, off), (ext_hbm, ext), (occ_hbm, occ), (pot_hbm, pot)])
    ]
    load_c.start()
    load_d.start()
    load_z.start()
    for copy in small:
        copy.start()
    load_e.start()

    barrier = pltpu.get_barrier_semaphore()
    for ds, db in AROUND:
        pl.semaphore_signal(barrier, 1, device_id=device(-ds, -db), device_id_type=MESH)
        if ds == 0:
            pl.semaphore_signal(barrier, 1, device_id=device(ds, db), device_id_type=MESH)
        else:

            @pl.when(s + ds < 16)
            def _(ds=ds, db=db):
                pl.semaphore_signal(barrier, 1, device_id=device(ds, db), device_id_type=MESH)

    core = lax.rem(s, 2)
    partner = (s + 1 - 2 * core, j)
    pl.semaphore_signal(barrier, 1, device_id=partner, device_id_type=MESH)
    wrapped = (s < 2).astype(jnp.int32)

    def enter():
        pl.semaphore_wait(barrier, 11 - wrapped)

        @pl.when(s >= 14)
        def _():
            pl.semaphore_signal(late, 1, device_id=device(2, 0), device_id_type=MESH)

    for copy in small:
        copy.wait()
    dz = [off[0, f] & (CZ - 1) for f in range(FD)]
    dy = [off[1, f] & (RY - 1) for f in range(FD)]
    ox = [off[2, f] for f in range(FD)]
    turn = [(ox[f] + 32 * dy[f]) & 127 for f in range(FD)]
    for y in range(RY):
        row = pot[:, y * NX : (y + 1) * NX]
        row = pltpu.roll(row, 32 * (y % 4), 1) if y % 4 else row
        seen[0, 0, y] = row
        window[y, 0:CZ] = row
    zero = jnp.zeros((CZ, NX), F32)
    for f in range(FD):
        for k in range(12):
            for part in range(4):
                if k in (0, 1, 10, 11) or part in (0, 3):
                    at = (f * 12 + k) * 32 + part * 8
                    term[at : at + 8] = zero

    load_d.wait()
    for k in range(3):
        h, l = split(kd[k])
        tiles[k, 0] = h
        tiles[k, 1] = l
    load_z.wait()
    for source, target in ((0, zd), (1, ze)):
        h, l = split(zm[source])
        target[:, 0:128] = h
        target[:, 128:256] = l
    load_c.wait()
    for t in range(4):
        h, l = split(coef[:, t * LT : (t + 1) * LT])
        pair[t, 0:128] = h
        pair[t, 128:256] = l

    @pl.when(s >= 14)
    def _():
        enter()

    lane = lax.broadcasted_iota(jnp.int32, (BZ, NX), 1)
    layer = lax.broadcasted_iota(jnp.int32, (BZ, NX), 0)
    lane_x = lane & 31
    lane_y = lane >> 5
    lanes = lax.broadcasted_iota(jnp.int32, (WZ, NX), 1)
    group = [((lanes - ox[f]) & 127) >> 5 for f in range(FD)]
    first = [[(f * 12 + ((q - dy[f] + 8) >> 2)) * 32 + 8 - dz[f] for q in range(4)] for f in range(FD)]

    def remote(source, target, k, to):
        return pltpu.make_async_remote_copy(
            source, target, send_sem.at[k], recv_sem.at[k], device_id=to, device_id_type=MESH
        )

    def density_pair(db):
        return remote(acc.at[db, 1], got.at[db, 1], db, partner)

    def density_plane(ds, db):
        return remote(acc.at[db, ds], got.at[db, ds], 5 + 2 * (db - 1) + ds // 2, device(0, db))

    def density_layers():
        return remote(acc.at[0, 2], got.at[0, 2], 13, device(2, 0))

    def potential_layers():
        return remote(seen.at[0, 0], seen.at[0, 2], 14, device(-2, 0))

    def potential_plane(ds, db):
        return remote(seen.at[0, ds], seen.at[db, ds], 15 + 2 * (db - 1) + ds // 2, device(0, -db))

    def potential_pair(db):
        return remote(seen.at[db, 2 - 2 * core], seen.at[db, 1], 23 + db, partner)

    def merge(db):
        density_pair(db).wait_recv()
        for y in range(RY):
            acc[db, 2 - 2 * core, y] += got[db, 1, y]
        if db > 0:
            density_plane(2, db).start()

    def forward_low():
        for db in (1, 2, 3, 4):
            potential_plane(0, db).start()

    def forward_high():
        potential_layers().wait_recv()
        for db in (1, 2, 3, 4):
            potential_plane(2, db).start()

    @pl.when(s >= 14)
    def _():
        potential_layers().start()
        forward_low()

    for t in (3, 2, 1, 0):
        plane = None
        for step in (-1, 0, 1):
            if not 0 <= t + step < 4:
                continue
            both = dot(pair[t + step], tiles[step + 1, 0])
            part = both[0:128] + both[128:256] + dot(pair[t + step, 0:128], tiles[step + 1, 1])
            plane = part if plane is None else plane + part
        gh, gl = split(plane)
        full = dot(zd[...], jnp.concatenate([gh, gh], axis=0)) + dot(zd[:, 0:128], gl)
        for f in range(FD):
            live_zx = (layer < ext[0, f]) & (lane_x < ext[2, f])
            weight = occ[f].astype(F32)
            for half in range(2):
                k = 2 * t + half
                live = live_zx & (lane_y < ext[1, f] - 4 * k)
                value = jnp.where(live, full[f * BZ : (f + 1) * BZ, half * NX : (half + 1) * NX], 0.0)
                orb[f, k] = value
                at = (f * 12 + k + 2) * 32 + 8
                term[at : at + BZ] = pltpu.roll(weight * (value * value), turn[f], 1)
        for db in (t + 1,) if t else (1, 0):
            for q in range(4):
                totals = [jnp.zeros((WZ, NX), F32)] * 2
                for f in range(FD):
                    mine = group[f] == q
                    for m in range(2):
                        rows = term[pl.ds(first[f][q] + 32 * (2 * db + m), WZ), :]
                        totals[m] = totals[m] + jnp.where(mine, rows, 0.0)
                for m in range(2):
                    for ds in range(3):
                        acc[db, ds, q + 4 * m] = totals[m][ds * CZ : (ds + 1) * CZ]
            if db == 4:

                @pl.when(s < 14)
                def _():
                    enter()

                @pl.when((s >= 2) & (s < 14))
                def _():
                    potential_layers().start()

            density_pair(db).start()
            if db < 4:
                merge(db + 1)

    @pl.when(s < 14)
    def _():
        forward_low()
        for db in (4, 3, 2, 1):
            density_plane(0, db).start()
        forward_high()

    @pl.when(s < 2)
    def _():
        pl.semaphore_wait(late, 1)
        potential_layers().start()

    merge(0)
    for db in (4, 3, 2, 1):
        density_plane(2, db).wait_recv()
    for y in range(RY):
        acc[0, 2, y] = (acc[0, 2, y] + got[4, 2, y]) + (got[3, 2, y] + got[2, 2, y]) + got[1, 2, y]
    density_layers().start()

    @pl.when(s >= 14)
    def _():
        for db in (4, 3, 2, 1):
            density_plane(0, db).start()
        forward_high()

    potential_pair(0).start()
    for db in (1, 2, 3, 4):
        potential_plane(0, db).wait_recv()
        potential_plane(2, db).wait_recv()
        potential_pair(db).start()
    for db in range(5):
        potential_pair(db).wait_recv()
        for y in range(RY):
            for ds in range(3):
                if ds + db > 0:
                    window[RY * db + y, ds * CZ : (ds + 1) * CZ] = seen[db, ds, y]
    for f in range(FD):
        mine = ((((lane - ox[f]) & 127) >> 5) - dy[f]) & 3
        back_turn = (128 - turn[f]) & 127
        for k in range(8):
            box = None
            for g in range(4):
                rows = window[4 * k + g + dy[f], pl.ds(dz[f], BZ), :]
                box = rows if g == 0 else jnp.where(mine == g, rows, box)
            prod[f * BZ : (f + 1) * BZ, k * NX : (k + 1) * NX] = pltpu.roll(box, back_turn, 1) * orb[f, k]
    load_e.wait()
    for t in range(4):
        ph, p_low = split(prod[:, t * LT : (t + 1) * LT])
        back = dot(ze[...], jnp.concatenate([ph, ph], axis=0)) + dot(ze[:, 0:128], p_low)
        h, l = split(back)
        high[t * 128 : (t + 1) * 128] = h
        low[t * 128 : (t + 1) * 128] = l
    plane_filter(high, low, ke, grid)
    for t in range(4):
        app[:, t * LT : (t + 1) * LT] = grid[t * 128 : (t + 1) * 128]

    for db in (4, 3, 2, 1):
        density_plane(0, db).wait_recv()
    density_layers().wait_recv()
    for y in range(RY):
        total = acc[0, 0, y] + got[0, 2, y]
        for db in (4, 3, 2, 1):
            total = total + got[db, 0, y]
        den[:, y * NX : (y + 1) * NX] = pltpu.roll(total, 128 - 32 * (y % 4), 1) if y % 4 else total
    for db in (1, 2, 3, 4):
        for ds in (0, 2):
            density_plane(ds, db).wait_send()
            potential_plane(ds, db).wait_send()
    for db in range(5):
        density_pair(db).wait_send()
        potential_pair(db).wait_send()
    density_layers().wait_send()
    potential_layers().wait_send()


def per_device(coefficients, offsets, extents, occupancy, potential):
    hbm = pl.BlockSpec(memory_space=pltpu.HBM)
    whole = pl.BlockSpec(memory_space=pltpu.VMEM)
    app, den = pl.pallas_call(
        work,
        out_shape=(
            pltpu.VMEM((FD * BZ, BY * BX), F32),
            pltpu.VMEM((CZ, RY * NX), F32),
        ),
        in_specs=[hbm] * 8,
        out_specs=(whole, whole),
        scratch_shapes=[
            pltpu.VMEM((128, 1024), F32),
            pltpu.VMEM((3, LT, LT), F32),
            pltpu.VMEM((3, LT, LT), F32),
            pltpu.VMEM((2, 128, 128), F32),
            pltpu.VMEM((3, 2, LT, LT), BF16),
            pltpu.VMEM((4, 256, LT), BF16),
            pltpu.VMEM((512, LT), BF16),
            pltpu.VMEM((512, LT), BF16),
            pltpu.VMEM((512, LT), F32),
            pltpu.VMEM((128, 256), BF16),
            pltpu.VMEM((128, 256), BF16),
            pltpu.VMEM((FD, 8, BZ, NX), F32),
            pltpu.VMEM((FD * 12 * 32, NX), F32),
            pltpu.VMEM((5, 3, RY, CZ, NX), F32),
            pltpu.VMEM((WY, WZ, NX), F32),
            pltpu.VMEM((5, 3, RY, CZ, NX), F32),
            pltpu.VMEM((5, 3, RY, CZ, NX), F32),
            pltpu.VMEM((128, 1024), F32),
            pltpu.SMEM((3, FD), jnp.int32),
            pltpu.SMEM((3, FD), jnp.int32),
            pltpu.SMEM((FD,), jnp.int32),
            pltpu.VMEM((CZ, RY * NX), F32),
            pltpu.SemaphoreType.DMA((9,)),
            pltpu.SemaphoreType.DMA((28,)),
            pltpu.SemaphoreType.DMA((28,)),
            pltpu.SemaphoreType.REGULAR,
        ],
        compiler_params=pltpu.CompilerParams(
            collective_id=0, has_side_effects=True, vmem_limit_bytes=63 * 1024 * 1024
        ),
        name="local_potential",
    )(
        offsets.T,
        extents.T,
        occupancy,
        coefficients.reshape(FD * BZ, BY * BX),
        potential,
        jnp.asarray(plane_tiles(False)),
        jnp.asarray(plane_tiles(True)),
        jnp.asarray(layer_matrices()),
    )
    return den, app.reshape(FD, BZ, BY * BX)


def solution(mesh):
    in_specs = (
        P(("slab", "func"), None, None),
        P(("slab", "func"), None),
        P(("slab", "func"), None),
        P(("slab", "func")),
        P("slab", "func"),
    )
    out_specs = (P("slab", "func"), P(("slab", "func"), None, None))
    return jax.shard_map(
        per_device, mesh=mesh, in_specs=in_specs, out_specs=out_specs, check_vma=False
    )
```

```python
import jax
import jax.numpy as jnp
import numpy as np
from jax import lax
from jax.experimental import pallas as pl
from jax.experimental.pallas import tpu as pltpu
from jax.sharding import PartitionSpec as P

BZ = 16
BY = 32
BX = 32
CZ = 8
RY = 8
NX = 128
FD = 8
WZ = 24
WY = 40
LT = 256
MESH = pl.DeviceIdType.MESH
F32 = jnp.float32
BF16 = jnp.bfloat16
STRAIGHT = (0,)
AROUND = [(2, 0)] + [(0, db) for db in (4, 3, 2, 1)]

magic_taps = np.array(
    [
        8.433424733352934e-07,
        -1.290557201342061e-05,
        8.76298447621056e-05,
        -0.00030158038132690465,
        0.001747237136729939,
        -0.009420470302010804,
        0.023738214637249424,
        0.0612625895831208,
        0.9940415697834004,
        -0.06048952891969835,
        -0.021030251609303816,
        0.013372634148547948,
        -0.0034412814449349387,
        0.0004944322768868992,
        -5.185986881173433e-05,
        2.7273449291197967e-06,
    ]
).astype(np.float32)


def tap(distance):
    inside = (distance >= -8) & (distance <= 7)
    return np.where(inside, magic_taps[np.clip(distance + 8, 0, 15)], 0.0).astype(np.float64)


def plane_tiles(backward):
    row = np.arange(LT)[:, None]
    col = np.arange(LT)[None, :]
    tiles = []
    for step in (-1, 0, 1):
        if backward:
            along_y = tap(col // BX - row // BX - 8 * step)
            along_x = tap(col % BX - row % BX)
        else:
            along_y = tap(8 * step + row // BX - col // BX)
            along_x = tap(row % BX - col % BX)
        full = along_y * along_x
        tiles.append(full.astype(np.float32))
    return np.stack(tiles)


def split(value):
    high = value.astype(BF16)
    return high, (value - high.astype(F32)).astype(BF16)


def dot(a, b):
    return jnp.dot(a, b, preferred_element_type=F32)


def plane_filter(high, low, tiles, out):
    def pair(first, last, step):
        big, small = split(tiles[step + 1])
        return dot(high[first:last], big) + dot(low[first:last], big) + dot(high[first:last], small)

    out[...] = pair(0, 512, 0)
    out[0:384] += pair(128, 512, 1)
    out[128:512] += pair(0, 384, -1)


def layer_matrices():
    row = np.arange(FD * BZ)[:, None]
    col = np.arange(FD * BZ)[None, :]
    full = np.where(row // BZ == col // BZ, tap(col - row), 0.0).astype(np.float32)
    return np.stack([full, full.T])


def work(
    off_hbm, ext_hbm, occ_hbm, coef_hbm, pot_hbm, kd_hbm, ke_hbm, z_hbm, app, den,
    coef, kd, ke, zm, tiles, pair, high, low, grid, zd, ze, orb, term, seen, window, acc, got, prod,
    off, ext, occ, pot, load_sem, send_sem, recv_sem, late,
):
    s = lax.axis_index("slab")
    j = lax.axis_index("func")

    def device(a, b):
        return (lax.rem(s + a + 16, 16), lax.rem(j + b + 32, 32))

    load_c = pltpu.make_async_copy(coef_hbm, coef, load_sem.at[0])
    load_d = pltpu.make_async_copy(kd_hbm, kd, load_sem.at[1])
    load_z = pltpu.make_async_copy(z_hbm, zm, load_sem.at[2])
    load_e = pltpu.make_async_copy(ke_hbm, ke, load_sem.at[3])
    small = [
        pltpu.make_async_copy(source, target, load_sem.at[5 + k])
        for k, (source, target) in enumerate([(off_hbm, off), (ext_hbm, ext), (occ_hbm, occ), (pot_hbm, pot)])
    ]
    load_c.start()
    load_d.start()
    load_z.start()
    for copy in small:
        copy.start()
    load_e.start()

    barrier = pltpu.get_barrier_semaphore()
    for ds, db in AROUND:
        pl.semaphore_signal(barrier, 1, device_id=device(-ds, -db), device_id_type=MESH)
        if ds == 0:
            pl.semaphore_signal(barrier, 1, device_id=device(ds, db), device_id_type=MESH)
        else:

            @pl.when(s + ds < 16)
            def _(ds=ds, db=db):
                pl.semaphore_signal(barrier, 1, device_id=device(ds, db), device_id_type=MESH)

    for db in (4, 3, 2, 1):
        pl.semaphore_signal(barrier, 1, device_id=device(-2, -db), device_id_type=MESH)
    for db in STRAIGHT:
        pl.semaphore_signal(barrier, 1, device_id=device(-1, -db), device_id_type=MESH)
    core = lax.rem(s, 2)
    partner = (s + 1 - 2 * core, j)
    pl.semaphore_signal(barrier, 1, device_id=partner, device_id_type=MESH)
    wrapped = (s < 2).astype(jnp.int32)

    def enter():
        pl.semaphore_wait(barrier, 15 + len(STRAIGHT) - wrapped)

        @pl.when(s >= 14)
        def _():
            pl.semaphore_signal(late, 1, device_id=device(2, 0), device_id_type=MESH)

    for copy in small:
        copy.wait()
    dz = [off[0, f] & (CZ - 1) for f in range(FD)]
    dy = [off[1, f] & (RY - 1) for f in range(FD)]
    ox = [off[2, f] for f in range(FD)]
    turn = [(ox[f] + 32 * dy[f]) & 127 for f in range(FD)]
    for y in range(RY):
        row = pot[:, y * NX : (y + 1) * NX]
        row = pltpu.roll(row, 32 * (y % 4), 1) if y % 4 else row
        seen[0, 0, y] = row
        window[y, 0:CZ] = row
    zero = jnp.zeros((CZ, NX), F32)
    for f in range(FD):
        for k in range(12):
            for part in range(4):
                if k in (0, 1, 10, 11) or part in (0, 3):
                    at = (f * 12 + k) * 32 + part * 8
                    term[at : at + 8] = zero

    load_d.wait()
    for k in range(3):
        h, l = split(kd[k])
        tiles[k, 0] = h
        tiles[k, 1] = l
    load_z.wait()
    for source, target in ((0, zd), (1, ze)):
        h, l = split(zm[source])
        target[:, 0:128] = h
        target[:, 128:256] = l
    load_c.wait()
    for t in range(4):
        h, l = split(coef[:, t * LT : (t + 1) * LT])
        pair[t, 0:128] = h
        pair[t, 128:256] = l

    @pl.when(s >= 14)
    def _():
        enter()

    lane = lax.broadcasted_iota(jnp.int32, (BZ, NX), 1)
    layer = lax.broadcasted_iota(jnp.int32, (BZ, NX), 0)
    lane_x = lane & 31
    lane_y = lane >> 5
    lanes = lax.broadcasted_iota(jnp.int32, (WZ, NX), 1)
    group = [((lanes - ox[f]) & 127) >> 5 for f in range(FD)]
    first = [[(f * 12 + ((q - dy[f] + 8) >> 2)) * 32 + 8 - dz[f] for q in range(4)] for f in range(FD)]

    def remote(source, target, k, to):
        return pltpu.make_async_remote_copy(
            source, target, send_sem.at[k], recv_sem.at[k], device_id=to, device_id_type=MESH
        )

    def density_pair(db):
        to = device(1, db) if db in STRAIGHT else partner
        return remote(acc.at[db, 1], got.at[db, 1], db, to)

    def density_low(db):
        return remote(acc.at[db, 0], got.at[db, 0], 5 + db, device(0, db))

    def density_high(db):
        return remote(acc.at[db, 2], got.at[db, 2], 9 + db if db else 5, device(2, db))

    def potential_layers():
        return remote(seen.at[0, 0], seen.at[0, 2], 14, device(-2, 0))

    def potential_plane(ds, db):
        return remote(seen.at[0, ds], seen.at[db, ds], 15 + 2 * (db - 1) + ds // 2, device(0, -db))

    def potential_pair(db):
        return remote(seen.at[db, 2 - 2 * core], seen.at[db, 1], 23 + db, partner)

    def merge(db):
        if db in STRAIGHT:
            return
        density_pair(db).wait_recv()
        for y in range(RY):
            acc[db, 2 - 2 * core, y] += got[db, 1, y]
        density_high(db).start()

    def forward_low():
        for db in (1, 2, 3, 4):
            potential_plane(0, db).start()

    def forward_high():
        potential_layers().wait_recv()
        for db in (1, 2, 3, 4):
            potential_plane(2, db).start()

    @pl.when(s >= 14)
    def _():
        potential_layers().start()
        forward_low()

    def filtered(t):
        plane = None
        for step in (-1, 0, 1):
            if not 0 <= t + step < 4:
                continue
            both = dot(pair[t + step], tiles[step + 1, 0])
            part = both[0:128] + both[128:256] + dot(pair[t + step, 0:128], tiles[step + 1, 1])
            plane = part if plane is None else plane + part
        gh, gl = split(plane)
        return dot(zd[...], jnp.concatenate([gh, gh], axis=0)) + dot(zd[:, 0:128], gl)

    ahead = filtered(3)
    for t in (3, 2, 1, 0):
        full = ahead
        if t:
            ahead = filtered(t - 1)
        for f in range(FD):
            live_zx = (layer < ext[0, f]) & (lane_x < ext[2, f])
            weight = occ[f].astype(F32)
            for half in range(2):
                k = 2 * t + half
                live = live_zx & (lane_y < ext[1, f] - 4 * k)
                value = jnp.where(live, full[f * BZ : (f + 1) * BZ, half * NX : (half + 1) * NX], 0.0)
                orb[f, k] = value
                at = (f * 12 + k + 2) * 32 + 8
                term[at : at + BZ] = pltpu.roll(weight * (value * value), turn[f], 1)
        for db in (t + 1,) if t else (1, 0):
            for q in range(4):
                totals = [jnp.zeros((WZ, NX), F32)] * 2
                for f in range(FD):
                    mine = group[f] == q
                    for m in range(2):
                        rows = term[pl.ds(first[f][q] + 32 * (2 * db + m), WZ), :]
                        totals[m] = totals[m] + jnp.where(mine, rows, 0.0)
                for m in range(2):
                    for ds in range(3):
                        acc[db, ds, q + 4 * m] = totals[m][ds * CZ : (ds + 1) * CZ]
            if db == 4:

                @pl.when(s < 14)
                def _():
                    enter()

                @pl.when((s >= 2) & (s < 14))
                def _():
                    potential_layers().start()

            if db in STRAIGHT:
                density_high(db).start()
            density_pair(db).start()
            if db < 4:
                merge(db + 1)

    @pl.when(s < 14)
    def _():
        forward_low()

    merge(0)
    for db in (4, 3, 2, 1):
        density_low(db).start()
    forward_high()

    @pl.when(s < 2)
    def _():
        pl.semaphore_wait(late, 1)
        potential_layers().start()

    potential_pair(0).start()
    for db in (1, 2, 3, 4):
        potential_plane(0, db).wait_recv()
        potential_plane(2, db).wait_recv()
        potential_pair(db).start()
    for db in range(5):
        potential_pair(db).wait_recv()
        for y in range(RY):
            for ds in range(3):
                if ds + db > 0:
                    window[RY * db + y, ds * CZ : (ds + 1) * CZ] = seen[db, ds, y]
    for f in range(FD):
        mine = ((((lane - ox[f]) & 127) >> 5) - dy[f]) & 3
        back_turn = (128 - turn[f]) & 127
        for k in range(8):
            box = None
            for g in range(4):
                rows = window[4 * k + g + dy[f], pl.ds(dz[f], BZ), :]
                box = rows if g == 0 else jnp.where(mine == g, rows, box)
            prod[f * BZ : (f + 1) * BZ, k * NX : (k + 1) * NX] = pltpu.roll(box, back_turn, 1) * orb[f, k]
    load_e.wait()
    for t in range(4):
        ph, p_low = split(prod[:, t * LT : (t + 1) * LT])
        back = dot(ze[...], jnp.concatenate([ph, ph], axis=0)) + dot(ze[:, 0:128], p_low)
        h, l = split(back)
        high[t * 128 : (t + 1) * 128] = h
        low[t * 128 : (t + 1) * 128] = l
    plane_filter(high, low, ke, grid)
    for t in range(4):
        app[:, t * LT : (t + 1) * LT] = grid[t * 128 : (t + 1) * 128]

    for db in (4, 3, 2, 1):
        density_low(db).wait_recv()
    lows = []
    for y in range(RY):
        total = acc[0, 0, y]
        for db in (4, 3, 2, 1):
            total = total + got[db, 0, y]
        lows.append(total)
    for db in (4, 3, 2, 1, 0):
        density_high(db).wait_recv()
        if db in STRAIGHT:
            density_pair(db).wait_recv()
    for y in range(RY):
        total = lows[y]
        for db in (4, 3, 2, 1, 0):
            total = total + got[db, 2, y]
        for db in STRAIGHT:
            total = total + got[db, 1, y]
        den[:, y * NX : (y + 1) * NX] = pltpu.roll(total, 128 - 32 * (y % 4), 1) if y % 4 else total
    for db in (1, 2, 3, 4):
        density_low(db).wait_send()
        for ds in (0, 2):
            potential_plane(ds, db).wait_send()
    for db in range(5):
        density_high(db).wait_send()
        density_pair(db).wait_send()
        potential_pair(db).wait_send()
    potential_layers().wait_send()


def per_device(coefficients, offsets, extents, occupancy, potential):
    hbm = pl.BlockSpec(memory_space=pltpu.HBM)
    whole = pl.BlockSpec(memory_space=pltpu.VMEM)
    app, den = pl.pallas_call(
        work,
        out_shape=(
            pltpu.VMEM((FD * BZ, BY * BX), F32),
            pltpu.VMEM((CZ, RY * NX), F32),
        ),
        in_specs=[hbm] * 8,
        out_specs=(whole, whole),
        scratch_shapes=[
            pltpu.VMEM((128, 1024), F32),
            pltpu.VMEM((3, LT, LT), F32),
            pltpu.VMEM((3, LT, LT), F32),
            pltpu.VMEM((2, 128, 128), F32),
            pltpu.VMEM((3, 2, LT, LT), BF16),
            pltpu.VMEM((4, 256, LT), BF16),
            pltpu.VMEM((512, LT), BF16),
            pltpu.VMEM((512, LT), BF16),
            pltpu.VMEM((512, LT), F32),
            pltpu.VMEM((128, 256), BF16),
            pltpu.VMEM((128, 256), BF16),
            pltpu.VMEM((FD, 8, BZ, NX), F32),
            pltpu.VMEM((FD * 12 * 32, NX), F32),
            pltpu.VMEM((5, 3, RY, CZ, NX), F32),
            pltpu.VMEM((WY, WZ, NX), F32),
            pltpu.VMEM((5, 3, RY, CZ, NX), F32),
            pltpu.VMEM((5, 3, RY, CZ, NX), F32),
            pltpu.VMEM((128, 1024), F32),
            pltpu.SMEM((3, FD), jnp.int32),
            pltpu.SMEM((3, FD), jnp.int32),
            pltpu.SMEM((FD,), jnp.int32),
            pltpu.VMEM((CZ, RY * NX), F32),
            pltpu.SemaphoreType.DMA((9,)),
            pltpu.SemaphoreType.DMA((28,)),
            pltpu.SemaphoreType.DMA((28,)),
            pltpu.SemaphoreType.REGULAR,
        ],
        compiler_params=pltpu.CompilerParams(
            collective_id=0, has_side_effects=True, vmem_limit_bytes=63 * 1024 * 1024
        ),
        name="local_potential",
    )(
        offsets.T,
        extents.T,
        occupancy,
        coefficients.reshape(FD * BZ, BY * BX),
        potential,
        jnp.asarray(plane_tiles(False)),
        jnp.asarray(plane_tiles(True)),
        jnp.asarray(layer_matrices()),
    )
    return den, app.reshape(FD, BZ, BY * BX)


def solution(mesh):
    in_specs = (
        P(("slab", "func"), None, None),
        P(("slab", "func"), None),
        P(("slab", "func"), None),
        P(("slab", "func")),
        P("slab", "func"),
    )
    out_specs = (P("slab", "func"), P(("slab", "func"), None, None))
    return jax.shard_map(
        per_device, mesh=mesh, in_specs=in_specs, out_specs=out_specs, check_vma=False
    )
```

```python
import jax
import jax.numpy as jnp
import numpy as np
from jax import lax
from jax.experimental import pallas as pl
from jax.experimental.pallas import tpu as pltpu
from jax.sharding import PartitionSpec as P

BZ = 16
BY = 32
BX = 32
CZ = 8
RY = 8
NX = 128
FD = 8
WZ = 24
WY = 40
LT = 256
MESH = pl.DeviceIdType.MESH
F32 = jnp.float32
BF16 = jnp.bfloat16
STRAIGHT = (0,)
AROUND = [(2, 0)] + [(0, db) for db in (4, 3, 2, 1)]

magic_taps = np.array(
    [
        8.433424733352934e-07,
        -1.290557201342061e-05,
        8.76298447621056e-05,
        -0.00030158038132690465,
        0.001747237136729939,
        -0.009420470302010804,
        0.023738214637249424,
        0.0612625895831208,
        0.9940415697834004,
        -0.06048952891969835,
        -0.021030251609303816,
        0.013372634148547948,
        -0.0034412814449349387,
        0.0004944322768868992,
        -5.185986881173433e-05,
        2.7273449291197967e-06,
    ]
).astype(np.float32)


def tap(distance):
    inside = (distance >= -8) & (distance <= 7)
    return np.where(inside, magic_taps[np.clip(distance + 8, 0, 15)], 0.0).astype(np.float64)


def plane_tiles(backward):
    row = np.arange(LT)[:, None]
    col = np.arange(LT)[None, :]
    tiles = []
    for step in (-1, 0, 1):
        if backward:
            along_y = tap(col // BX - row // BX - 8 * step)
            along_x = tap(col % BX - row % BX)
        else:
            along_y = tap(8 * step + row // BX - col // BX)
            along_x = tap(row % BX - col % BX)
        full = along_y * along_x
        tiles.append(full.astype(np.float32))
    return np.stack(tiles)


def split(value):
    high = value.astype(BF16)
    return high, (value - high.astype(F32)).astype(BF16)


def dot(a, b):
    return jnp.dot(a, b, preferred_element_type=F32)


def plane_filter(high, low, tiles, out):
    def pair(first, last, step):
        big, small = split(tiles[step + 1])
        return dot(high[first:last], big) + dot(low[first:last], big) + dot(high[first:last], small)

    out[...] = pair(0, 512, 0)
    out[0:384] += pair(128, 512, 1)
    out[128:512] += pair(0, 384, -1)


def layer_matrices():
    row = np.arange(FD * BZ)[:, None]
    col = np.arange(FD * BZ)[None, :]
    full = np.where(row // BZ == col // BZ, tap(col - row), 0.0).astype(np.float32)
    return np.stack([full, full.T])


def work(
    off_hbm, ext_hbm, occ_hbm, coef_hbm, pot_hbm, kd_hbm, ke_hbm, z_hbm, app, den,
    coef, kd, ke, zm, tiles, pair, high, low, grid, zd, ze, orb, term, seen, window, acc, got, prod,
    off, ext, occ, pot, load_sem, send_sem, recv_sem, late,
):
    s = lax.axis_index("slab")
    j = lax.axis_index("func")

    def device(a, b):
        return (lax.rem(s + a + 16, 16), lax.rem(j + b + 32, 32))

    load_c = pltpu.make_async_copy(coef_hbm, coef, load_sem.at[0])
    load_d = pltpu.make_async_copy(kd_hbm, kd, load_sem.at[1])
    load_z = pltpu.make_async_copy(z_hbm, zm, load_sem.at[2])
    load_e = pltpu.make_async_copy(ke_hbm, ke, load_sem.at[3])
    small = [
        pltpu.make_async_copy(source, target, load_sem.at[5 + k])
        for k, (source, target) in enumerate([(off_hbm, off), (ext_hbm, ext), (occ_hbm, occ), (pot_hbm, pot)])
    ]
    load_c.start()
    load_d.start()
    load_z.start()
    for copy in small:
        copy.start()
    load_e.start()

    barrier = pltpu.get_barrier_semaphore()
    for ds, db in AROUND:
        pl.semaphore_signal(barrier, 1, device_id=device(-ds, -db), device_id_type=MESH)
        if ds == 0:
            pl.semaphore_signal(barrier, 1, device_id=device(ds, db), device_id_type=MESH)
        else:

            @pl.when(s + ds < 16)
            def _(ds=ds, db=db):
                pl.semaphore_signal(barrier, 1, device_id=device(ds, db), device_id_type=MESH)

    for db in (4, 3, 2, 1):
        pl.semaphore_signal(barrier, 1, device_id=device(-2, -db), device_id_type=MESH)
    for db in STRAIGHT:
        pl.semaphore_signal(barrier, 1, device_id=device(-1, -db), device_id_type=MESH)
    core = lax.rem(s, 2)
    partner = (s + 1 - 2 * core, j)
    pl.semaphore_signal(barrier, 1, device_id=partner, device_id_type=MESH)
    wrapped = (s < 2).astype(jnp.int32)

    def enter():
        pl.semaphore_wait(barrier, 15 + len(STRAIGHT) - wrapped)

        @pl.when(s >= 14)
        def _():
            pl.semaphore_signal(late, 1, device_id=device(2, 0), device_id_type=MESH)

    for copy in small:
        copy.wait()
    dz = [off[0, f] & (CZ - 1) for f in range(FD)]
    dy = [off[1, f] & (RY - 1) for f in range(FD)]
    ox = [off[2, f] for f in range(FD)]
    turn = [(ox[f] + 32 * dy[f]) & 127 for f in range(FD)]
    for y in range(RY):
        row = pot[:, y * NX : (y + 1) * NX]
        row = pltpu.roll(row, 32 * (y % 4), 1) if y % 4 else row
        seen[0, 0, y] = row
        window[y, 0:CZ] = row
    zero = jnp.zeros((CZ, NX), F32)
    for f in range(FD):
        for k in range(12):
            for part in range(4):
                if k in (0, 1, 10, 11) or part in (0, 3):
                    at = (f * 12 + k) * 32 + part * 8
                    term[at : at + 8] = zero

    load_d.wait()
    for k in range(3):
        h, l = split(kd[k])
        tiles[k, 0] = h
        tiles[k, 1] = l
    load_z.wait()
    for source, target in ((0, zd), (1, ze)):
        h, l = split(zm[source])
        target[:, 0:128] = h
        target[:, 128:256] = l
    load_c.wait()
    for t in range(4):
        h, l = split(coef[:, t * LT : (t + 1) * LT])
        pair[t, 0:128] = h
        pair[t, 128:256] = l

    lane = lax.broadcasted_iota(jnp.int32, (BZ, NX), 1)
    layer = lax.broadcasted_iota(jnp.int32, (BZ, NX), 0)
    lane_x = lane & 31
    lane_y = lane >> 5
    lanes = lax.broadcasted_iota(jnp.int32, (WZ, NX), 1)
    group = [((lanes - ox[f]) & 127) >> 5 for f in range(FD)]
    first = [[(f * 12 + ((q - dy[f] + 8) >> 2)) * 32 + 8 - dz[f] for q in range(4)] for f in range(FD)]

    def remote(source, target, k, to):
        return pltpu.make_async_remote_copy(
            source, target, send_sem.at[k], recv_sem.at[k], device_id=to, device_id_type=MESH
        )

    def density_pair(db):
        to = device(1, db) if db in STRAIGHT else partner
        return remote(acc.at[db, 1], got.at[db, 1], db, to)

    def density_low(db):
        return remote(acc.at[db, 0], got.at[db, 0], 5 + db, device(0, db))

    def density_high(db):
        return remote(acc.at[db, 2], got.at[db, 2], 9 + db if db else 5, device(2, db))

    def potential_layers():
        return remote(seen.at[0, 0], seen.at[0, 2], 14, device(-2, 0))

    def potential_plane(ds, db):
        return remote(seen.at[0, ds], seen.at[db, ds], 15 + 2 * (db - 1) + ds // 2, device(0, -db))

    def potential_pair(db):
        return remote(seen.at[db, 2 - 2 * core], seen.at[db, 1], 23 + db, partner)

    def merge(db):
        if db in STRAIGHT:
            return
        density_pair(db).wait_recv()
        for y in range(RY):
            acc[db, 2 - 2 * core, y] += got[db, 1, y]
        density_high(db).start()

    def forward_low():
        for db in (1, 2, 3, 4):
            potential_plane(0, db).start()

    def forward_high():
        potential_layers().wait_recv()
        for db in (1, 2, 3, 4):
            potential_plane(2, db).start()

    def filtered(t):
        plane = None
        for step in (-1, 0, 1):
            if not 0 <= t + step < 4:
                continue
            both = dot(pair[t + step], tiles[step + 1, 0])
            part = both[0:128] + both[128:256] + dot(pair[t + step, 0:128], tiles[step + 1, 1])
            plane = part if plane is None else plane + part
        gh, gl = split(plane)
        return dot(zd[...], jnp.concatenate([gh, gh], axis=0)) + dot(zd[:, 0:128], gl)

    ahead = filtered(3)
    for t in (3, 2, 1, 0):
        full = ahead
        if t:
            ahead = filtered(t - 1)
        for f in range(FD):
            live_zx = (layer < ext[0, f]) & (lane_x < ext[2, f])
            weight = occ[f].astype(F32)
            for half in range(2):
                k = 2 * t + half
                live = live_zx & (lane_y < ext[1, f] - 4 * k)
                value = jnp.where(live, full[f * BZ : (f + 1) * BZ, half * NX : (half + 1) * NX], 0.0)
                orb[f, k] = value
                at = (f * 12 + k + 2) * 32 + 8
                term[at : at + BZ] = pltpu.roll(weight * (value * value), turn[f], 1)
        for db in (t + 1,) if t else (1, 0):
            for q in range(4):
                totals = [jnp.zeros((WZ, NX), F32)] * 2
                for f in range(FD):
                    mine = group[f] == q
                    for m in range(2):
                        rows = term[pl.ds(first[f][q] + 32 * (2 * db + m), WZ), :]
                        totals[m] = totals[m] + jnp.where(mine, rows, 0.0)
                for m in range(2):
                    for ds in range(3):
                        acc[db, ds, q + 4 * m] = totals[m][ds * CZ : (ds + 1) * CZ]
            if db == 4:

                enter()

                @pl.when(s >= 2)
                def _():
                    potential_layers().start()

            if db in STRAIGHT:
                density_high(db).start()
            density_pair(db).start()
            if db < 4:
                merge(db + 1)

    merge(0)
    for db in (4, 3, 2, 1):
        density_low(db).start()

    forward_low()
    forward_high()

    @pl.when(s < 2)
    def _():
        pl.semaphore_wait(late, 1)
        potential_layers().start()

    potential_pair(0).start()
    for db in (1, 2, 3, 4):
        potential_plane(0, db).wait_recv()
        potential_plane(2, db).wait_recv()
        potential_pair(db).start()
    for db in range(5):
        potential_pair(db).wait_recv()
        for y in range(RY):
            for ds in range(3):
                if ds + db > 0:
                    window[RY * db + y, ds * CZ : (ds + 1) * CZ] = seen[db, ds, y]
    for f in range(FD):
        mine = ((((lane - ox[f]) & 127) >> 5) - dy[f]) & 3
        back_turn = (128 - turn[f]) & 127
        for k in range(8):
            box = None
            for g in range(4):
                rows = window[4 * k + g + dy[f], pl.ds(dz[f], BZ), :]
                box = rows if g == 0 else jnp.where(mine == g, rows, box)
            prod[f * BZ : (f + 1) * BZ, k * NX : (k + 1) * NX] = pltpu.roll(box, back_turn, 1) * orb[f, k]
    load_e.wait()
    for t in range(4):
        ph, p_low = split(prod[:, t * LT : (t + 1) * LT])
        back = dot(ze[...], jnp.concatenate([ph, ph], axis=0)) + dot(ze[:, 0:128], p_low)
        h, l = split(back)
        high[t * 128 : (t + 1) * 128] = h
        low[t * 128 : (t + 1) * 128] = l
    plane_filter(high, low, ke, grid)
    for t in range(4):
        app[:, t * LT : (t + 1) * LT] = grid[t * 128 : (t + 1) * 128]

    for db in (4, 3, 2, 1):
        density_low(db).wait_recv()
    lows = []
    for y in range(RY):
        total = acc[0, 0, y]
        for db in (4, 3, 2, 1):
            total = total + got[db, 0, y]
        lows.append(total)
    for db in (4, 3, 2, 1, 0):
        density_high(db).wait_recv()
        if db in STRAIGHT:
            density_pair(db).wait_recv()
    for y in range(RY):
        total = lows[y]
        for db in (4, 3, 2, 1, 0):
            total = total + got[db, 2, y]
        for db in STRAIGHT:
            total = total + got[db, 1, y]
        den[:, y * NX : (y + 1) * NX] = pltpu.roll(total, 128 - 32 * (y % 4), 1) if y % 4 else total
    for db in (1, 2, 3, 4):
        density_low(db).wait_send()
        for ds in (0, 2):
            potential_plane(ds, db).wait_send()
    for db in range(5):
        density_high(db).wait_send()
        density_pair(db).wait_send()
        potential_pair(db).wait_send()
    potential_layers().wait_send()


def per_device(coefficients, offsets, extents, occupancy, potential):
    hbm = pl.BlockSpec(memory_space=pltpu.HBM)
    whole = pl.BlockSpec(memory_space=pltpu.VMEM)
    app, den = pl.pallas_call(
        work,
        out_shape=(
            pltpu.VMEM((FD * BZ, BY * BX), F32),
            pltpu.VMEM((CZ, RY * NX), F32),
        ),
        in_specs=[hbm] * 8,
        out_specs=(whole, whole),
        scratch_shapes=[
            pltpu.VMEM((128, 1024), F32),
            pltpu.VMEM((3, LT, LT), F32),
            pltpu.VMEM((3, LT, LT), F32),
            pltpu.VMEM((2, 128, 128), F32),
            pltpu.VMEM((3, 2, LT, LT), BF16),
            pltpu.VMEM((4, 256, LT), BF16),
            pltpu.VMEM((512, LT), BF16),
            pltpu.VMEM((512, LT), BF16),
            pltpu.VMEM((512, LT), F32),
            pltpu.VMEM((128, 256), BF16),
            pltpu.VMEM((128, 256), BF16),
            pltpu.VMEM((FD, 8, BZ, NX), F32),
            pltpu.VMEM((FD * 12 * 32, NX), F32),
            pltpu.VMEM((5, 3, RY, CZ, NX), F32),
            pltpu.VMEM((WY, WZ, NX), F32),
            pltpu.VMEM((5, 3, RY, CZ, NX), F32),
            pltpu.VMEM((5, 3, RY, CZ, NX), F32),
            pltpu.VMEM((128, 1024), F32),
            pltpu.SMEM((3, FD), jnp.int32),
            pltpu.SMEM((3, FD), jnp.int32),
            pltpu.SMEM((FD,), jnp.int32),
            pltpu.VMEM((CZ, RY * NX), F32),
            pltpu.SemaphoreType.DMA((9,)),
            pltpu.SemaphoreType.DMA((28,)),
            pltpu.SemaphoreType.DMA((28,)),
            pltpu.SemaphoreType.REGULAR,
        ],
        compiler_params=pltpu.CompilerParams(
            collective_id=0, has_side_effects=True, vmem_limit_bytes=63 * 1024 * 1024
        ),
        name="local_potential",
    )(
        offsets.T,
        extents.T,
        occupancy,
        coefficients.reshape(FD * BZ, BY * BX),
        potential,
        jnp.asarray(plane_tiles(False)),
        jnp.asarray(plane_tiles(True)),
        jnp.asarray(layer_matrices()),
    )
    return den, app.reshape(FD, BZ, BY * BX)


def solution(mesh):
    in_specs = (
        P(("slab", "func"), None, None),
        P(("slab", "func"), None),
        P(("slab", "func"), None),
        P(("slab", "func")),
        P("slab", "func"),
    )
    out_specs = (P("slab", "func"), P(("slab", "func"), None, None))
    return jax.shard_map(
        per_device, mesh=mesh, in_specs=in_specs, out_specs=out_specs, check_vma=False
    )
```

```python
import jax
import jax.numpy as jnp
import numpy as np
from jax import lax
from jax.experimental import pallas as pl
from jax.experimental.pallas import tpu as pltpu
from jax.sharding import PartitionSpec as P

BZ = 16
BY = 32
BX = 32
CZ = 8
RY = 8
NX = 128
FD = 8
WZ = 24
WY = 40
LT = 256
MESH = pl.DeviceIdType.MESH
F32 = jnp.float32
BF16 = jnp.bfloat16
STRAIGHT = (0,)
AROUND = [(2, 0)] + [(0, db) for db in (4, 3, 2, 1)]

magic_taps = np.array(
    [
        8.433424733352934e-07,
        -1.290557201342061e-05,
        8.76298447621056e-05,
        -0.00030158038132690465,
        0.001747237136729939,
        -0.009420470302010804,
        0.023738214637249424,
        0.0612625895831208,
        0.9940415697834004,
        -0.06048952891969835,
        -0.021030251609303816,
        0.013372634148547948,
        -0.0034412814449349387,
        0.0004944322768868992,
        -5.185986881173433e-05,
        2.7273449291197967e-06,
    ]
).astype(np.float32)


def tap(distance):
    inside = (distance >= -8) & (distance <= 7)
    return np.where(inside, magic_taps[np.clip(distance + 8, 0, 15)], 0.0).astype(np.float64)


def plane_tiles(backward):
    row = np.arange(LT)[:, None]
    col = np.arange(LT)[None, :]
    tiles = []
    for step in (-1, 0, 1):
        if backward:
            along_y = tap(col // BX - row // BX - 8 * step)
            along_x = tap(col % BX - row % BX)
        else:
            along_y = tap(8 * step + row // BX - col // BX)
            along_x = tap(row % BX - col % BX)
        full = along_y * along_x
        tiles.append(full.astype(np.float32))
    return np.stack(tiles)


def split(value):
    high = value.astype(BF16)
    return high, (value - high.astype(F32)).astype(BF16)


def dot(a, b):
    return jnp.dot(a, b, preferred_element_type=F32)


def plane_filter(high, low, tiles, out):
    def pair(first, last, step):
        big, small = split(tiles[step + 1])
        return dot(high[first:last], big) + dot(low[first:last], big) + dot(high[first:last], small)

    out[...] = pair(0, 512, 0)
    out[0:384] += pair(128, 512, 1)
    out[128:512] += pair(0, 384, -1)


def layer_matrices():
    row = np.arange(FD * BZ)[:, None]
    col = np.arange(FD * BZ)[None, :]
    full = np.where(row // BZ == col // BZ, tap(col - row), 0.0).astype(np.float32)
    return np.stack([full, full.T])


def work(
    off_hbm, ext_hbm, occ_hbm, coef_hbm, pot_hbm, kd_hbm, ke_hbm, z_hbm, app, den,
    coef, kd, ke, zm, tiles, pair, high, low, grid, zd, ze, orb, term, seen, window, acc, got, prod,
    off, ext, occ, pot, load_sem, send_sem, recv_sem, late,
):
    s = lax.axis_index("slab")
    j = lax.axis_index("func")

    def device(a, b):
        return (lax.rem(s + a + 16, 16), lax.rem(j + b + 32, 32))

    load_c = pltpu.make_async_copy(coef_hbm, coef, load_sem.at[0])
    load_d = pltpu.make_async_copy(kd_hbm, kd, load_sem.at[1])
    load_z = pltpu.make_async_copy(z_hbm, zm, load_sem.at[2])
    load_e = pltpu.make_async_copy(ke_hbm, ke, load_sem.at[3])
    small = [
        pltpu.make_async_copy(source, target, load_sem.at[5 + k])
        for k, (source, target) in enumerate([(off_hbm, off), (ext_hbm, ext), (occ_hbm, occ), (pot_hbm, pot)])
    ]
    load_c.start()
    load_d.start()
    load_z.start()
    for copy in small:
        copy.start()
    load_e.start()

    barrier = pltpu.get_barrier_semaphore()
    for ds, db in AROUND:
        pl.semaphore_signal(barrier, 1, device_id=device(-ds, -db), device_id_type=MESH)
        if ds == 0:
            pl.semaphore_signal(barrier, 1, device_id=device(ds, db), device_id_type=MESH)
        else:

            @pl.when(s + ds < 16)
            def _(ds=ds, db=db):
                pl.semaphore_signal(barrier, 1, device_id=device(ds, db), device_id_type=MESH)

    for db in (4, 3, 2, 1):
        pl.semaphore_signal(barrier, 1, device_id=device(-2, -db), device_id_type=MESH)
    for db in STRAIGHT:
        pl.semaphore_signal(barrier, 1, device_id=device(-1, -db), device_id_type=MESH)
    core = lax.rem(s, 2)
    partner = (s + 1 - 2 * core, j)
    pl.semaphore_signal(barrier, 1, device_id=partner, device_id_type=MESH)
    wrapped = (s < 2).astype(jnp.int32)

    def enter():
        pl.semaphore_wait(barrier, 15 + len(STRAIGHT) - wrapped)

        @pl.when(s >= 14)
        def _():
            pl.semaphore_signal(late, 1, device_id=device(2, 0), device_id_type=MESH)

    for copy in small:
        copy.wait()
    dz = [off[0, f] & (CZ - 1) for f in range(FD)]
    dy = [off[1, f] & (RY - 1) for f in range(FD)]
    ox = [off[2, f] for f in range(FD)]
    turn = [(ox[f] + 32 * dy[f]) & 127 for f in range(FD)]
    for y in range(RY):
        row = pot[:, y * NX : (y + 1) * NX]
        row = pltpu.roll(row, 32 * (y % 4), 1) if y % 4 else row
        seen[0, 0, y] = row
        window[y, 0:CZ] = row
    zero = jnp.zeros((CZ, NX), F32)
    for f in range(FD):
        for k in range(12):
            for part in range(4):
                if k in (0, 1, 10, 11) or part in (0, 3):
                    at = (f * 12 + k) * 32 + part * 8
                    term[at : at + 8] = zero

    load_d.wait()
    for k in range(3):
        h, l = split(kd[k])
        tiles[k, 0] = h
        tiles[k, 1] = l
    load_z.wait()
    for source, target in ((0, zd), (1, ze)):
        h, l = split(zm[source])
        target[:, 0:128] = h
        target[:, 128:256] = l
    load_c.wait()
    for t in range(4):
        h, l = split(coef[:, t * LT : (t + 1) * LT])
        pair[t, 0:128] = h
        pair[t, 128:256] = l

    lane = lax.broadcasted_iota(jnp.int32, (BZ, NX), 1)
    layer = lax.broadcasted_iota(jnp.int32, (BZ, NX), 0)
    lane_x = lane & 31
    lane_y = lane >> 5
    lanes = lax.broadcasted_iota(jnp.int32, (WZ, NX), 1)
    group = [((lanes - ox[f]) & 127) >> 5 for f in range(FD)]
    first = [[(f * 12 + ((q - dy[f] + 8) >> 2)) * 32 + 8 - dz[f] for q in range(4)] for f in range(FD)]

    def remote(source, target, k, to):
        return pltpu.make_async_remote_copy(
            source, target, send_sem.at[k], recv_sem.at[k], device_id=to, device_id_type=MESH
        )

    def density_pair(db):
        to = device(1, db) if db in STRAIGHT else partner
        return remote(acc.at[db, 1], got.at[db, 1], db, to)

    def density_low(db):
        return remote(acc.at[db, 0], got.at[db, 0], 5 + db, device(0, db))

    def density_high(db):
        return remote(acc.at[db, 2], got.at[db, 2], 9 + db if db else 5, device(2, db))

    def potential_layers():
        return remote(seen.at[0, 0], seen.at[0, 2], 14, device(-2, 0))

    def potential_plane(ds, db):
        return remote(seen.at[0, ds], seen.at[db, ds], 15 + 2 * (db - 1) + ds // 2, device(0, -db))

    def potential_pair(db):
        return remote(seen.at[db, 2 - 2 * core], seen.at[db, 1], 23 + db, partner)

    def merge(db):
        if db in STRAIGHT:
            return
        density_pair(db).wait_recv()
        for y in range(RY):
            acc[db, 2 - 2 * core, y] += got[db, 1, y]
        density_high(db).start()

    def forward_low():
        for db in (1, 2, 3, 4):
            potential_plane(0, db).start()

    def forward_high():
        potential_layers().wait_recv()
        for db in (1, 2, 3, 4):
            potential_plane(2, db).start()

    def filtered(t):
        plane = rest = None
        for step in (-1, 0, 1):
            if not 0 <= t + step < 4:
                continue
            near = dot(pair[t + step, 0:128], tiles[step + 1, 0]) + dot(pair[t + step, 0:128], tiles[step + 1, 1])
            far = dot(pair[t + step, 128:256], tiles[step + 1, 0])
            plane = near if plane is None else plane + near
            rest = far if rest is None else rest + far
        gh, gl = split(plane + rest)
        return dot(zd[...], jnp.concatenate([gh, gh], axis=0)) + dot(zd[:, 0:128], gl)

    ahead = filtered(3)
    for t in (3, 2, 1, 0):
        full = ahead
        if t:
            ahead = filtered(t - 1)
        for f in range(FD):
            live_zx = (layer < ext[0, f]) & (lane_x < ext[2, f])
            weight = occ[f].astype(F32)
            for half in range(2):
                k = 2 * t + half
                live = live_zx & (lane_y < ext[1, f] - 4 * k)
                value = jnp.where(live, full[f * BZ : (f + 1) * BZ, half * NX : (half + 1) * NX], 0.0)
                orb[f, k] = value
                at = (f * 12 + k + 2) * 32 + 8
                term[at : at + BZ] = pltpu.roll(weight * (value * value), turn[f], 1)
        for db in (t + 1,) if t else (1, 0):
            for q in range(4):
                totals = [jnp.zeros((WZ, NX), F32)] * 2
                for f in range(FD):
                    mine = group[f] == q
                    for m in range(2):
                        rows = term[pl.ds(first[f][q] + 32 * (2 * db + m), WZ), :]
                        totals[m] = totals[m] + jnp.where(mine, rows, 0.0)
                for m in range(2):
                    for ds in range(3):
                        acc[db, ds, q + 4 * m] = totals[m][ds * CZ : (ds + 1) * CZ]
            if db == 4:

                enter()

                @pl.when(s >= 2)
                def _():
                    potential_layers().start()

            if db in STRAIGHT:
                density_high(db).start()
            density_pair(db).start()
            if db < 4:
                merge(db + 1)

    merge(0)
    for db in (4, 3, 2, 1):
        density_low(db).start()

    forward_low()
    forward_high()

    @pl.when(s < 2)
    def _():
        pl.semaphore_wait(late, 1)
        potential_layers().start()

    potential_pair(0).start()
    for db in (1, 2, 3, 4):
        potential_plane(0, db).wait_recv()
        potential_plane(2, db).wait_recv()
        potential_pair(db).start()
    for db in range(5):
        potential_pair(db).wait_recv()
        for y in range(RY):
            for ds in range(3):
                if ds + db > 0:
                    window[RY * db + y, ds * CZ : (ds + 1) * CZ] = seen[db, ds, y]
    for f in range(FD):
        mine = ((((lane - ox[f]) & 127) >> 5) - dy[f]) & 3
        back_turn = (128 - turn[f]) & 127
        for k in range(8):
            box = None
            for g in range(4):
                rows = window[4 * k + g + dy[f], pl.ds(dz[f], BZ), :]
                box = rows if g == 0 else jnp.where(mine == g, rows, box)
            prod[f * BZ : (f + 1) * BZ, k * NX : (k + 1) * NX] = pltpu.roll(box, back_turn, 1) * orb[f, k]
    load_e.wait()
    for t in range(4):
        ph, p_low = split(prod[:, t * LT : (t + 1) * LT])
        back = dot(ze[...], jnp.concatenate([ph, ph], axis=0)) + dot(ze[:, 0:128], p_low)
        h, l = split(back)
        high[t * 128 : (t + 1) * 128] = h
        low[t * 128 : (t + 1) * 128] = l
    plane_filter(high, low, ke, grid)
    for t in range(4):
        app[:, t * LT : (t + 1) * LT] = grid[t * 128 : (t + 1) * 128]

    for db in (4, 3, 2, 1):
        density_low(db).wait_recv()
    lows = []
    for y in range(RY):
        total = acc[0, 0, y]
        for db in (4, 3, 2, 1):
            total = total + got[db, 0, y]
        lows.append(total)
    for db in (4, 3, 2, 1, 0):
        density_high(db).wait_recv()
        if db in STRAIGHT:
            density_pair(db).wait_recv()
    for y in range(RY):
        total = lows[y]
        for db in (4, 3, 2, 1, 0):
            total = total + got[db, 2, y]
        for db in STRAIGHT:
            total = total + got[db, 1, y]
        den[:, y * NX : (y + 1) * NX] = pltpu.roll(total, 128 - 32 * (y % 4), 1) if y % 4 else total
    for db in (1, 2, 3, 4):
        density_low(db).wait_send()
        for ds in (0, 2):
            potential_plane(ds, db).wait_send()
    for db in range(5):
        density_high(db).wait_send()
        density_pair(db).wait_send()
        potential_pair(db).wait_send()
    potential_layers().wait_send()


def per_device(coefficients, offsets, extents, occupancy, potential):
    hbm = pl.BlockSpec(memory_space=pltpu.HBM)
    whole = pl.BlockSpec(memory_space=pltpu.VMEM)
    app, den = pl.pallas_call(
        work,
        out_shape=(
            pltpu.VMEM((FD * BZ, BY * BX), F32),
            pltpu.VMEM((CZ, RY * NX), F32),
        ),
        in_specs=[hbm] * 8,
        out_specs=(whole, whole),
        scratch_shapes=[
            pltpu.VMEM((128, 1024), F32),
            pltpu.VMEM((3, LT, LT), F32),
            pltpu.VMEM((3, LT, LT), F32),
            pltpu.VMEM((2, 128, 128), F32),
            pltpu.VMEM((3, 2, LT, LT), BF16),
            pltpu.VMEM((4, 256, LT), BF16),
            pltpu.VMEM((512, LT), BF16),
            pltpu.VMEM((512, LT), BF16),
            pltpu.VMEM((512, LT), F32),
            pltpu.VMEM((128, 256), BF16),
            pltpu.VMEM((128, 256), BF16),
            pltpu.VMEM((FD, 8, BZ, NX), F32),
            pltpu.VMEM((FD * 12 * 32, NX), F32),
            pltpu.VMEM((5, 3, RY, CZ, NX), F32),
            pltpu.VMEM((WY, WZ, NX), F32),
            pltpu.VMEM((5, 3, RY, CZ, NX), F32),
            pltpu.VMEM((5, 3, RY, CZ, NX), F32),
            pltpu.VMEM((128, 1024), F32),
            pltpu.SMEM((3, FD), jnp.int32),
            pltpu.SMEM((3, FD), jnp.int32),
            pltpu.SMEM((FD,), jnp.int32),
            pltpu.VMEM((CZ, RY * NX), F32),
            pltpu.SemaphoreType.DMA((9,)),
            pltpu.SemaphoreType.DMA((28,)),
            pltpu.SemaphoreType.DMA((28,)),
            pltpu.SemaphoreType.REGULAR,
        ],
        compiler_params=pltpu.CompilerParams(
            collective_id=0, has_side_effects=True, vmem_limit_bytes=63 * 1024 * 1024
        ),
        name="local_potential",
    )(
        offsets.T,
        extents.T,
        occupancy,
        coefficients.reshape(FD * BZ, BY * BX),
        potential,
        jnp.asarray(plane_tiles(False)),
        jnp.asarray(plane_tiles(True)),
        jnp.asarray(layer_matrices()),
    )
    return den, app.reshape(FD, BZ, BY * BX)


def solution(mesh):
    in_specs = (
        P(("slab", "func"), None, None),
        P(("slab", "func"), None),
        P(("slab", "func"), None),
        P(("slab", "func")),
        P("slab", "func"),
    )
    out_specs = (P("slab", "func"), P(("slab", "func"), None, None))
    return jax.shard_map(
        per_device, mesh=mesh, in_specs=in_specs, out_specs=out_specs, check_vma=False
    )
```
